32 devices in a mesh: seq: 16 (over z, y, x), dp: 2 (over core).
Axes of the slice: x: 2, y: 2, z: 4, core: 2. Of those that a mesh axis runs over, the one named last changes fastest.
Arguments:
- queries: bfloat16 [2, 6144, 1024], P('dp', 'seq'), may hold values from -6 to 6
- keys: bfloat16 [2, 6144, 1024], P('dp', 'seq'), may hold values from -6 to 6
- values: bfloat16 [2, 6144, 1024], P('dp', 'seq'), may hold values from -6 to 6
- out_grad: bfloat16 [2, 6144, 1024], P('dp', 'seq'), may hold values from -6 to 6
- proj_weight: bfloat16 [1024, 1024], replicated, may hold values from -0.1875 to 0.1875
- lengths: int32 [2, 32], P('dp'), may hold values from 1 to 768, 6144 in all within a row
Outputs:
- query_grads: bfloat16 [2, 6144, 1024], P('dp', 'seq')
- key_grads: bfloat16 [2, 6144, 1024], P('dp', 'seq')
- value_grads: bfloat16 [2, 6144, 1024], P('dp', 'seq')
- weight_grad: float32 [1024, 1024], P(('seq', 'dp'))
The draws below stay inside these ranges and needn't reach their ends.
Inputs may be any that keep to these rules, and one draw needn't show every extreme that they name: In each stream the 32 utterance lengths cover the 6144 frames end to end; the longest is exactly 768.
All inputs are finite; a program needn't handle non-finite values.
Results may differ from the reference program's by a relative error of at most 0.02.
Values may be sent and summed in bfloat16 or wider, within the bound.
A program may use at most 128 MiB of HBM per device.

```python
import math
import jax
import jax.numpy as jnp
import numpy as np
from jax import lax

D = 1024
HEADS = 8
WINDOW = 256
FRAMES_DEV = 384
FRAMES = 6144
STREAMS = 2
UTTS = 32
MOST = 768


def rough_base(key, spread):
    return spread * jax.random.truncated_normal(key, -3.0, 3.0, (STREAMS, FRAMES, D), jnp.float32)


def draw_queries(key, part):
    key = jax.random.fold_in(key, 1)
    return rough_base(key, 1.5).astype(jnp.bfloat16)


def draw_keys(key, part):
    key = jax.random.fold_in(key, 2)
    return rough_base(key, 1.5).astype(jnp.bfloat16)


def raised(entries, rng, source, target, blocks, factor):
    def block_of(position):
        return (jnp.arange(entries.shape[position]) // (entries.shape[position] // blocks)).reshape((-1,) + (1,) * (entries.ndim - 1 - position))

    first = jax.random.permutation(rng, blocks)[block_of(target)]
    far = (block_of(target) + blocks // 2) % blocks
    return jnp.where((block_of(source) == first) | (block_of(source) == far), factor * entries, entries)


def shard_levels(own_key, shape, cuts, smallest, top_value):
    level = 1.0
    for dim, parts in cuts:
        heights = jax.random.uniform(jax.random.fold_in(jax.random.fold_in(own_key, 6), dim), (parts,), jnp.float32, smallest / len(cuts), top_value / len(cuts))
        level = level * jnp.repeat(jnp.exp(heights), shape[dim] // parts).reshape((-1,) + (1,) * (len(shape) - 1 - dim))
    return level


def split_up(amount, total, bound, skew):
    portions = [(1 << 20) // math.isqrt(standing ** skew) + 1 for standing in range(2, amount + 1)]
    surplus, holding = total - bound - (amount - 1), [1] * (amount - 1)
    while surplus > 0:
        candidates = [i for i in range(amount - 1) if holding[i] < bound]
        pool, budget = sum([portions[i] for i in candidates]), surplus
        for i in candidates:
            addition = min(bound - holding[i], max(1, budget * portions[i] // pool), surplus)
            holding[i] = holding[i] + addition
            surplus = surplus - addition
    return np.array([bound] + holding)


def ragged(rng, count, total, most, skew):
    if count == 2:
        one = jax.random.randint(rng, (), max(1, total - most), min(most, total - 1) + 1)
        return jnp.stack([one, total - one])
    tallies = jnp.asarray(split_up(count, total, most, skew), jnp.int32)
    couples = (count - 1) // 2
    donor, sink = tallies[1:1 + 2 * couples:2], tallies[2:2 + 2 * couples:2]
    margin = jnp.minimum(donor - 1, most - sink)
    shifted = jax.random.randint(jax.random.fold_in(rng, 1), (couples,), 0, 1 << 20) % (margin + 1)
    tallies = tallies.at[1:1 + 2 * couples:2].set(donor - shifted).at[2:2 + 2 * couples:2].set(sink + shifted)
    return tallies[jax.random.permutation(jax.random.fold_in(rng, 2), count)]


def normal_values(own_key, shape, scale, most, cuts=(), held_as=jnp.bfloat16):
    gain = shard_levels(own_key, shape, cuts, -0.22, 0.18) if cuts else 1.0
    drawn = jax.random.normal(own_key, shape, jnp.float32) * scale * gain
    return jnp.minimum(jnp.maximum(drawn, -most), most).astype(held_as)


def noise_with(rng, shape, width, limit, split, heavy, held_as=jnp.bfloat16):
    entries = width * jax.random.normal(rng, shape, jnp.float32)
    if split:
        entries = entries * shard_levels(rng, shape, split, -0.22, 0.18)
    return jnp.clip(raised(entries, jax.random.fold_in(rng, 3), *heavy), -limit, limit).astype(held_as)


def setup_inputs(seed: int = 0) -> dict:
    splits = jax.random.split(jax.random.key(seed), 7)
    queries = draw_queries(jax.random.fold_in(splits[6], 71), 0)
    keys = draw_keys(jax.random.fold_in(splits[6], 71), 0)
    values = normal_values(splits[2], (STREAMS, FRAMES, D), 1.0, 6.0, ((0, 2), (1, 16)))
    out_grad = noise_with(splits[3], (STREAMS, FRAMES, D), 1.0, 6.0, ((0, 2), (1, 16)), (1, 2, 16, 2.0))
    proj_weight = normal_values(splits[4], (D, D), D ** -0.5, 0.1875)
    lengths = jax.vmap(lambda own: ragged(own, UTTS, FRAMES, MOST, 2))(jax.random.split(splits[5], STREAMS)).reshape((STREAMS, UTTS)).astype(jnp.int32)
    return {"queries": queries, "keys": keys, "values": values, "out_grad": out_grad, "proj_weight": proj_weight, "lengths": lengths}


NEG_FILL = -1e30


def inner_last(left, right):
    return lax.dot_general(left, right, (((1,), (1,)), ((), ())), preferred_element_type=jnp.float32)


def inner_first(left, right):
    return lax.dot_general(left, right, (((0,), (0,)), ((), ())), preferred_element_type=jnp.float32)


def segment_of(utter_ends, spots):
    return jnp.sum((utter_ends[None, :] <= spots[:, None]).astype(jnp.int32), axis=1)


def visible(query_spots, key_spots, utter_ends, grid_total, window):
    query_seg = segment_of(utter_ends, query_spots)
    key_seg = segment_of(utter_ends, key_spots)
    inside_query = (query_spots >= 0) & (query_spots < grid_total)
    inside_key = (key_spots >= 0) & (key_spots < grid_total)
    nearby = jnp.abs(query_spots[:, None] - key_spots[None, :]) <= window
    return nearby & (query_seg[:, None] == key_seg[None, :]) & inside_query[:, None] & inside_key[None, :]


def both_sides(query_head, key_head, value_head, grad_head, allowed):
    factor = query_head.shape[1] ** -0.5
    scores = inner_last(query_head, key_head) * factor
    scores = jnp.where(allowed, scores, NEG_FILL)
    row_peak = jnp.max(scores, axis=1, keepdims=True)
    exp_scores = jnp.exp(scores - row_peak)
    attn_probs = exp_scores / jnp.sum(exp_scores, axis=1, keepdims=True)
    probs_low = attn_probs.astype(jnp.bfloat16)
    attended = jnp.dot(probs_low, value_head, preferred_element_type=jnp.float32).astype(jnp.bfloat16)
    row_drift = jnp.sum(grad_head.astype(jnp.float32) * attended.astype(jnp.float32), axis=1, keepdims=True)
    value_grad = inner_first(probs_low, grad_head)
    prob_grad = inner_last(grad_head, value_head)
    score_grad = (attn_probs * (prob_grad - row_drift)).astype(jnp.bfloat16)
    query_grad = jnp.dot(score_grad, key_head, preferred_element_type=jnp.float32) * factor
    key_grad = inner_first(score_grad, query_head) * factor
    return query_grad, key_grad, value_grad, attended


def split_heads(block):
    rows_count = block.shape[0]
    return block.reshape(rows_count, HEADS, -1).transpose(1, 0, 2)


def join_heads(block):
    head_count, rows_count, head_width = block.shape
    return block.transpose(1, 0, 2).reshape(rows_count, head_count * head_width)


def reference(queries, keys, values, out_grad, proj_weight, lengths):
    span = FRAMES_DEV + 2 * WINDOW
    blocks = FRAMES // FRAMES_DEV
    query_list = []
    key_list = []
    value_list = []
    weight_grad = jnp.zeros((D, D), jnp.float32)
    for stream in range(STREAMS):
        grad_attn = jnp.dot(out_grad[stream], proj_weight, preferred_element_type=jnp.float32).astype(jnp.bfloat16)
        utter_ends = jnp.cumsum(lengths[stream]).astype(jnp.int32)
        key_pad = jnp.pad(keys[stream], ((WINDOW, WINDOW), (0, 0)))
        value_pad = jnp.pad(values[stream], ((WINDOW, WINDOW), (0, 0)))
        stream_queries = queries[stream]

        def advance(carry, block):
            key_acc, value_acc = carry
            first = block * FRAMES_DEV
            query_rows = lax.dynamic_slice_in_dim(stream_queries, first, FRAMES_DEV, 0)
            grad_rows = lax.dynamic_slice_in_dim(grad_attn, first, FRAMES_DEV, 0)
            key_rows = lax.dynamic_slice_in_dim(key_pad, first, span, 0)
            value_rows = lax.dynamic_slice_in_dim(value_pad, first, span, 0)
            own_spots = first + jnp.arange(FRAMES_DEV, dtype=jnp.int32)
            wide_spots = first - WINDOW + jnp.arange(span, dtype=jnp.int32)
            allowed = visible(own_spots, wide_spots, utter_ends, FRAMES, WINDOW)
            query_grad, key_grad, value_grad, attended = jax.vmap(both_sides, in_axes=(0, 0, 0, 0, None))(
                split_heads(query_rows), split_heads(key_rows), split_heads(value_rows), split_heads(grad_rows), allowed)
            key_acc = lax.dynamic_update_slice_in_dim(
                key_acc, lax.dynamic_slice_in_dim(key_acc, first, span, 0) + join_heads(key_grad), first, 0)
            value_acc = lax.dynamic_update_slice_in_dim(
                value_acc, lax.dynamic_slice_in_dim(value_acc, first, span, 0) + join_heads(value_grad), first, 0)
            return (key_acc, value_acc), (join_heads(query_grad).astype(jnp.bfloat16), join_heads(attended))

        zero_acc = jnp.zeros((FRAMES + 2 * WINDOW, D), jnp.float32)
        (key_acc, value_acc), (query_out, attended_all) = lax.scan(
            advance, (zero_acc, zero_acc), jnp.arange(blocks, dtype=jnp.int32))
        query_list.append(query_out.reshape(FRAMES, D))
        key_list.append(key_acc[WINDOW:WINDOW + FRAMES].astype(jnp.bfloat16))
        value_list.append(value_acc[WINDOW:WINDOW + FRAMES].astype(jnp.bfloat16))
        weight_grad = weight_grad + inner_first(out_grad[stream], attended_all.reshape(FRAMES, D))
    return jnp.stack(query_list), jnp.stack(key_list), jnp.stack(value_list), weight_grad
```

```python
import functools

import jax
import jax.numpy as jnp
from jax import lax
from jax.experimental import pallas as pl
from jax.experimental.pallas import tpu as pltpu
from jax.sharding import PartitionSpec as P

HEADS = 8
WINDOW = 256
GROUP = 2
NEG_FILL = -1e30
MESH = pl.DeviceIdType.MESH


def dot(left, right, left_dim, right_dim):
    return lax.dot_general(
        left, right, (((left_dim,), (right_dim,)), ((), ())), preferred_element_type=jnp.float32
    )


def iota(shape, dim):
    return lax.broadcasted_iota(jnp.int32, shape, dim)


def fill_bias(bias, lengths_ref, me, frames):
    utts = lengths_ref.shape[1]
    lens = lengths_ref[...].astype(jnp.float32)
    upto = iota((utts, utts), 1) <= iota((utts, utts), 0)
    ends_col = jnp.sum(jnp.where(upto, lens, 0.0), axis=1, keepdims=True)
    same = iota((utts, utts), 1) == iota((utts, utts), 0)
    ends_row = jnp.sum(jnp.where(same, ends_col, 0.0), axis=0, keepdims=True)
    wide = bias.shape[1]
    last = ends_row[:, utts - 1 :]
    first = me * frames
    query_spots = first + iota((frames, 1), 0)
    key_spots = first - WINDOW + iota((1, wide), 1)
    query_at = query_spots.astype(jnp.float32)
    key_at = key_spots.astype(jnp.float32)
    query_seg = jnp.sum(jnp.where(ends_row <= query_at, 1.0, 0.0), axis=1, keepdims=True)
    key_seg = jnp.sum(jnp.where(ends_col <= key_at, 1.0, 0.0), axis=0, keepdims=True)
    key_seg = jnp.where((key_at >= 0.0) & (key_at < last), key_seg, -1.0)
    step = 128
    for r in range(0, frames, step):
        near = jnp.abs(query_at[r : r + step] - key_at) <= float(WINDOW)
        seen = near & (query_seg[r : r + step] == key_seg)
        bias[r : r + step, :] = jnp.where(seen, 0.0, NEG_FILL)


def kernel(
    n, inside,
    q_ref, k_ref, v_ref, g_ref, w_ref, lengths_ref,
    dq_ref, dk_ref, dv_ref, wg_ref,
    bias, ga, gt, att, key_acc, value_acc,
    halo_l, halo_r, out_l, out_r, ret_l, ret_r,
    halo_send, halo_recv, ret_send, ret_recv,
    *scatter,
):
    me = lax.axis_index("seq")
    core = lax.axis_index("dp")
    frames, width = q_ref.shape
    head = width // HEADS
    cols = GROUP * head
    groups = HEADS // GROUP
    factor = head ** (-0.5)
    has_l = me > 0
    has_r = me < n - 1
    left = jnp.maximum(me - 1, 0)
    right = jnp.minimum(me + 1, n - 1)
    if inside:
        x, y = lax.rem(me, 2), lax.rem(me // 2, 2)
        z0, z1 = lax.rem(me // 4, 2), me // 8
        partners = (
            (me, 1 - core),
            (me + 2 - 4 * y, core),
            (me + 4 - 8 * z0, core),
            (me + 8 - 16 * z1, core),
            (me + 1 - 2 * x, core),
        )
    else:
        partners = ()

    barrier = pltpu.get_barrier_semaphore()

    @pl.when(has_l)
    def _():
        pl.semaphore_signal(barrier, inc=1, device_id=(left, core), device_id_type=MESH)

    @pl.when(has_r)
    def _():
        pl.semaphore_signal(barrier, inc=1, device_id=(right, core), device_id_type=MESH)

    for partner in partners:
        pl.semaphore_signal(barrier, inc=1, device_id=partner, device_id_type=MESH)
    greeted = jnp.where(has_l, 1, 0) + jnp.where(has_r, 1, 0) + len(partners)
    pl.semaphore_wait(barrier, greeted)

    def halo_copy(which, side, g):
        src = (k_ref, v_ref)[which]
        rows = pl.ds(0, WINDOW) if side == 0 else pl.ds(frames - WINDOW, WINDOW)
        return pltpu.make_async_remote_copy(
            src_ref=src.at[rows, pl.ds(pl.multiple_of(g * cols, cols), cols)],
            dst_ref=(halo_r, halo_l)[side].at[which, g],
            send_sem=halo_send.at[which, side, g],
            recv_sem=halo_recv.at[which, side, g],
            device_id=((left, right)[side], core),
            device_id_type=MESH,
        )

    def ret_copy(which, side, g):
        return pltpu.make_async_remote_copy(
            src_ref=(out_l, out_r)[side].at[which, g],
            dst_ref=(ret_r, ret_l)[side].at[which, g],
            send_sem=ret_send.at[which, side, g],
            recv_sem=ret_recv.at[which, side, g],
            device_id=((left, right)[side], core),
            device_id_type=MESH,
        )

    def start_halos(g, _):
        @pl.when(has_l)
        def _():
            halo_copy(0, 0, g).start()
            halo_copy(1, 0, g).start()

        @pl.when(has_r)
        def _():
            halo_copy(0, 1, g).start()
            halo_copy(1, 1, g).start()

        return 0

    lax.fori_loop(0, groups, start_halos, 0)

    @pl.when(jnp.logical_not(has_l))
    def _():
        halo_l[...] = jnp.zeros_like(halo_l)
        ret_l[...] = jnp.zeros_like(ret_l)

    @pl.when(jnp.logical_not(has_r))
    def _():
        halo_r[...] = jnp.zeros_like(halo_r)
        ret_r[...] = jnp.zeros_like(ret_r)

    fill_bias(bias, lengths_ref, me, frames)
    gt[...] = g_ref[...].T

    def project(g, _):
        at = pl.ds(pl.multiple_of(g * cols, cols), cols)
        ga[:, at] = dot(g_ref[...], w_ref[:, at], 1, 0).astype(jnp.bfloat16)
        return 0

    lax.fori_loop(0, groups, project, 0)

    def one_group(g, _):
        @pl.when(has_l)
        def _():
            halo_copy(0, 1, g).wait_recv()
            halo_copy(1, 1, g).wait_recv()

        @pl.when(has_r)
        def _():
            halo_copy(0, 0, g).wait_recv()
            halo_copy(1, 0, g).wait_recv()

        for part in range(GROUP):
            at = pl.ds(pl.multiple_of(g * cols + part * head, head), head)
            inner = slice(part * head, (part + 1) * head)
            q = q_ref[:, at]
            grad = ga[:, at]
            key = jnp.concatenate([halo_l[0, g, :, inner], k_ref[:, at], halo_r[0, g, :, inner]], axis=0)
            value = jnp.concatenate([halo_l[1, g, :, inner], v_ref[:, at], halo_r[1, g, :, inner]], axis=0)
            scores = dot(q, key, 1, 1) * factor + bias[...]
            peak = jnp.max(scores, axis=1, keepdims=True)
            raised = jnp.exp(scores - peak)
            probs = raised * (1.0 / jnp.sum(raised, axis=1, keepdims=True))
            low = probs.astype(jnp.bfloat16)
            attended = dot(low, value, 1, 0).astype(jnp.bfloat16)
            att[:, at] = attended
            drift = jnp.sum(
                grad.astype(jnp.float32) * attended.astype(jnp.float32), axis=1, keepdims=True
            )
            value_grad = dot(low, grad, 0, 0)
            score_grad = (probs * (dot(grad, value, 1, 1) - drift)).astype(jnp.bfloat16)
            dq_ref[:, at] = (dot(score_grad, key, 1, 0) * factor).astype(jnp.bfloat16)
            key_grad = dot(score_grad, q, 0, 0) * factor
            for which, total, acc in ((0, key_grad, key_acc), (1, value_grad, value_acc)):
                out_l[which, g, :, inner] = total[:WINDOW].astype(jnp.bfloat16)
                acc[:, at] = total[WINDOW : WINDOW + frames]
                out_r[which, g, :, inner] = total[WINDOW + frames :].astype(jnp.bfloat16)

        @pl.when(has_l)
        def _():
            ret_copy(0, 0, g).start()
            ret_copy(1, 0, g).start()

        @pl.when(has_r)
        def _():
            ret_copy(0, 1, g).start()
            ret_copy(1, 1, g).start()

        return 0

    lax.fori_loop(0, groups, one_group, 0)

    if inside:
        wg, sums, send0, recv0, send1, recv1, send2, recv2, send3, recv3, send4, recv4, sc_send, sc_recv = scatter
        sends = (send0, send1, send2, send3, send4)
        recvs = (recv0, recv1, recv2, recv3, recv4)
    else:
        wg = wg_ref

    def weight(g, _):
        at = pl.ds(pl.multiple_of(g * cols, cols), cols)
        wg[:, at] = dot(gt[...], att[:, at], 1, 0)
        return 0

    lax.fori_loop(0, groups, weight, 0)

    if inside:
        block = wg_ref.shape[0]

        def exchange(step):
            return pltpu.make_async_remote_copy(
                src_ref=sends[step],
                dst_ref=recvs[step],
                send_sem=sc_send.at[step],
                recv_sem=sc_recv.at[step],
                device_id=partners[step],
                device_id_type=MESH,
            )

        def rows_of(s, c):
            return pl.ds(pl.multiple_of((s * 2 + c) * block, block), block)

        def pack0(s, _):
            send0[s] = wg[rows_of(s, 1 - core), :].astype(jnp.bfloat16)
            return 0

        lax.fori_loop(0, n, pack0, 0)
        exchange(0).start()
        exchange(0).wait_recv()

        def add0(s, _):
            sums[s] = wg[rows_of(s, core), :] + recv0[s].astype(jnp.float32)
            return 0

        lax.fori_loop(0, n, add0, 0)

        spots = (
            (8, lambda i, b: (i // 2) * 4 + b * 2 + lax.rem(i, 2), y),
            (4, lambda i, b: (i // 2) * 8 + b * 4 + y * 2 + lax.rem(i, 2), z0),
            (2, lambda i, b: b * 8 + z0 * 4 + y * 2 + i, z1),
            (1, lambda i, b: z1 * 8 + z0 * 4 + y * 2 + b + i * 0, x),
        )
        for t, (count, spot, bit) in enumerate(spots, 1):
            def pack(i, _):
                sends[t][i] = sums[spot(i, 1 - bit)].astype(jnp.bfloat16)
                return 0

            lax.fori_loop(0, count, pack, 0)
            exchange(t).start()
            exchange(t).wait_recv()

            def add(i, _):
                at = spot(i, bit)
                sums[at] = sums[at] + recvs[t][i].astype(jnp.float32)
                return 0

            lax.fori_loop(0, count, add, 0)
        wg_ref[...] = sums[me]
        for t in range(len(partners)):
            exchange(t).wait_send()

    def finish(g, _):
        @pl.when(has_l)
        def _():
            for which in range(2):
                ret_copy(which, 1, g).wait_recv()
                ret_copy(which, 0, g).wait_send()
                halo_copy(which, 0, g).wait_send()

        @pl.when(has_r)
        def _():
            for which in range(2):
                ret_copy(which, 0, g).wait_recv()
                ret_copy(which, 1, g).wait_send()
                halo_copy(which, 1, g).wait_send()

        at = pl.ds(pl.multiple_of(g * cols, cols), cols)
        for which, acc, out in ((0, key_acc, dk_ref), (1, value_acc, dv_ref)):
            total = acc[:, at]
            pad = jnp.zeros((frames - WINDOW, cols), jnp.float32)
            total = total + jnp.concatenate([ret_l[which, g].astype(jnp.float32), pad], axis=0)
            total = total + jnp.concatenate([pad, ret_r[which, g].astype(jnp.float32)], axis=0)
            out[:, at] = total.astype(jnp.bfloat16)
        return 0

    lax.fori_loop(0, groups, finish, 0)


def body(n, dp, queries, keys, values, out_grad, proj_weight, lengths):
    frames, width = queries.shape[1:]
    head = width // HEADS
    cols = GROUP * head
    groups = HEADS // GROUP
    inside = n == 16 and dp == 2
    block = width // (n * dp)
    wide = frames + 2 * WINDOW
    bf16, f32 = jnp.bfloat16, jnp.float32
    halo = pltpu.VMEM((2, groups, WINDOW, cols), bf16)
    sems = pltpu.SemaphoreType.DMA((2, 2, groups))
    scratch = [
        pltpu.VMEM((frames, wide), f32),
        pltpu.VMEM((frames, width), bf16),
        pltpu.VMEM((width, frames), bf16),
        pltpu.VMEM((frames, width), bf16),
        pltpu.VMEM((frames, width), f32),
        pltpu.VMEM((frames, width), f32),
        halo, halo, halo, halo, halo, halo,
        sems, sems, sems, sems,
    ]
    if inside:
        scratch += [pltpu.VMEM((width, width), f32), pltpu.VMEM((n, block, width), f32)]
        for count in (16, 8, 4, 2, 1):
            scratch += [pltpu.VMEM((count, block, width), bf16)] * 2
        scratch += [pltpu.SemaphoreType.DMA((5,))] * 2
    wg_shape = (block, width) if inside else (width, width)
    vmem = pl.BlockSpec(memory_space=pltpu.VMEM)
    dq, dk, dv, wg = pl.pallas_call(
        functools.partial(kernel, n, inside),
        out_shape=[jax.ShapeDtypeStruct((frames, width), bf16)] * 3
        + [jax.ShapeDtypeStruct(wg_shape, f32)],
        in_specs=[vmem] * 6,
        out_specs=[vmem] * 4,
        scratch_shapes=scratch,
        compiler_params=pltpu.CompilerParams(
            collective_id=0, has_side_effects=True, vmem_limit_bytes=56 * 1024 * 1024
        ),
    )(queries[0], keys[0], values[0], out_grad[0], proj_weight, lengths)
    if not inside:
        wg = lax.psum_scatter(wg, ("seq", "dp"), scatter_dimension=0, tiled=True)
    return dq[None], dk[None], dv[None], wg


def solution(mesh):
    rows = P("dp", "seq", None)
    return jax.shard_map(
        functools.partial(body, mesh.shape["seq"], mesh.shape["dp"]),
        mesh=mesh,
        in_specs=(rows, rows, rows, rows, P(), P("dp", None)),
        out_specs=(rows, rows, rows, P(("seq", "dp"), None)),
        check_vma=False,
    )
```

```python
import functools

import jax
import jax.numpy as jnp
from jax import lax
from jax.experimental import pallas as pl
from jax.experimental.pallas import tpu as pltpu
from jax.sharding import PartitionSpec as P

HEADS = 8
WINDOW = 256
GROUP = 2
NEG_FILL = -1e30
MESH = pl.DeviceIdType.MESH


def dot(left, right, left_dim, right_dim):
    return lax.dot_general(
        left, right, (((left_dim,), (right_dim,)), ((), ())), preferred_element_type=jnp.float32
    )


def iota(shape, dim):
    return lax.broadcasted_iota(jnp.int32, shape, dim)


def fill_bias(bias, lengths_ref, me, frames):
    utts = lengths_ref.shape[1]
    lens = lengths_ref[...].astype(jnp.float32)
    upto = iota((utts, utts), 1) <= iota((utts, utts), 0)
    ends_col = jnp.sum(jnp.where(upto, lens, 0.0), axis=1, keepdims=True)
    same = iota((utts, utts), 1) == iota((utts, utts), 0)
    ends_row = jnp.sum(jnp.where(same, ends_col, 0.0), axis=0, keepdims=True)
    wide = bias.shape[1]
    last = ends_row[:, utts - 1 :]
    first = me * frames
    query_spots = first + iota((frames, 1), 0)
    key_spots = first - WINDOW + iota((1, wide), 1)
    query_at = query_spots.astype(jnp.float32)
    key_at = key_spots.astype(jnp.float32)
    query_seg = jnp.sum(jnp.where(ends_row <= query_at, 1.0, 0.0), axis=1, keepdims=True)
    key_seg = jnp.sum(jnp.where(ends_col <= key_at, 1.0, 0.0), axis=0, keepdims=True)
    key_seg = jnp.where((key_at >= 0.0) & (key_at < last), key_seg, -1.0)
    step = 128
    for r in range(0, frames, step):
        near = jnp.abs(query_at[r : r + step] - key_at) <= float(WINDOW)
        seen = near & (query_seg[r : r + step] == key_seg)
        bias[r : r + step, :] = jnp.where(seen, 0.0, NEG_FILL)


def kernel(
    n, inside,
    q_ref, k_ref, v_ref, g_ref, w_ref, lengths_ref,
    dq_ref, dk_ref, dv_ref, wg_ref,
    bias, ga, gt, att, query_acc,
    grad_l, grad_r, halo_l, halo_r, out_l, out_r, ret_l, ret_r,
    local, final, part_l, part_r, got_l, got_r, done_l, done_r, told_l, told_r,
    grad_send, grad_recv, halo_send, halo_recv, ret_send, ret_recv,
    part_send, part_recv, done_send, done_recv,
    *scatter,
):
    me = lax.axis_index("seq")
    core = lax.axis_index("dp")
    frames, width = q_ref.shape
    head = width // HEADS
    cols = GROUP * head
    groups = HEADS // GROUP
    factor = head ** (-0.5)
    has_l = me > 0
    has_r = me < n - 1
    left = jnp.maximum(me - 1, 0)
    right = jnp.minimum(me + 1, n - 1)
    low_end, high_end = WINDOW, WINDOW + frames
    if inside:
        x, y = lax.rem(me, 2), lax.rem(me // 2, 2)
        z0, z1 = lax.rem(me // 4, 2), me // 8
        partners = (
            (me, 1 - core),
            (me + 2 - 4 * y, core),
            (me + 4 - 8 * z0, core),
            (me + 8 - 16 * z1, core),
            (me + 1 - 2 * x, core),
        )
    else:
        partners = ()

    barrier = pltpu.get_barrier_semaphore()

    @pl.when(has_l)
    def _():
        pl.semaphore_signal(barrier, inc=1, device_id=(left, core), device_id_type=MESH)

    @pl.when(has_r)
    def _():
        pl.semaphore_signal(barrier, inc=1, device_id=(right, core), device_id_type=MESH)

    for partner in partners:
        pl.semaphore_signal(barrier, inc=1, device_id=partner, device_id_type=MESH)
    greeted = jnp.where(has_l, 1, 0) + jnp.where(has_r, 1, 0) + len(partners)
    pl.semaphore_wait(barrier, greeted)

    edges = (pl.ds(0, WINDOW), pl.ds(frames - WINDOW, WINDOW))

    def copy(side, src, dst, send, recv):
        return pltpu.make_async_remote_copy(
            src_ref=src,
            dst_ref=dst,
            send_sem=send,
            recv_sem=recv,
            device_id=((left, right)[side], core),
            device_id_type=MESH,
        )

    def grad_copy(side, _):
        return copy(side, g_ref.at[edges[side], :], (grad_r, grad_l)[side],
                    grad_send.at[side], grad_recv.at[side])

    def halo_copy(side, g):
        at = pl.ds(pl.multiple_of(g * cols, cols), cols)
        return copy(side, q_ref.at[edges[side], at], (halo_r, halo_l)[side].at[g],
                    halo_send.at[side, g], halo_recv.at[side, g])

    def part_copy(side, b):
        return copy(side, (part_l, part_r)[side].at[b], (got_r, got_l)[side].at[b],
                    part_send.at[side, b], part_recv.at[side, b])

    def done_copy(side, b):
        return copy(side, (done_l, done_r)[side].at[b], (told_r, told_l)[side].at[b],
                    done_send.at[side, b], done_recv.at[side, b])

    def ret_copy(side, g):
        return copy(side, (out_l, out_r)[side].at[g], (ret_r, ret_l)[side].at[g],
                    ret_send.at[side, g], ret_recv.at[side, g])

    def start(make, i):
        @pl.when(has_l)
        def _():
            make(0, i).start()

        @pl.when(has_r)
        def _():
            make(1, i).start()

    def arrive(make, i):
        @pl.when(has_l)
        def _():
            make(1, i).wait_recv()

        @pl.when(has_r)
        def _():
            make(0, i).wait_recv()

    def sent(make, i):
        @pl.when(has_l)
        def _():
            make(0, i).wait_send()

        @pl.when(has_r)
        def _():
            make(1, i).wait_send()

    start(grad_copy, 0)

    def start_halos(g, _):
        start(halo_copy, g)
        return 0

    lax.fori_loop(0, groups, start_halos, 0)

    blank = jnp.where(iota((2, 16, WINDOW), 1) < 4, NEG_FILL, 0.0)

    @pl.when(jnp.logical_not(has_l))
    def _():
        for ref in (grad_l, halo_l, ret_l, told_l):
            ref[...] = jnp.zeros_like(ref)
        got_l[...] = blank

    @pl.when(jnp.logical_not(has_r))
    def _():
        for ref in (grad_r, halo_r, ret_r, told_r):
            ref[...] = jnp.zeros_like(ref)
        got_r[...] = blank

    fill_bias(bias, lengths_ref, me, frames)
    part_l[...] = jnp.zeros_like(part_l)
    part_r[...] = jnp.zeros_like(part_r)

    def project(ref, first, rows):
        gt[:, first : first + rows] = ref[...].T

        def some(g, _):
            at = pl.ds(pl.multiple_of(g * cols, cols), cols)
            ga[first : first + rows, at] = dot(ref[...], w_ref[:, at], 1, 0).astype(jnp.bfloat16)
            return 0

        lax.fori_loop(0, groups, some, 0)

    project(g_ref, low_end, frames)
    arrive(grad_copy, 0)
    project(grad_l, 0, WINDOW)
    project(grad_r, high_end, WINDOW)

    def operands(g, part):
        at = pl.ds(pl.multiple_of(g * cols + part * head, head), head)
        inner = slice(part * head, (part + 1) * head)
        query = jnp.concatenate([halo_l[g, :, inner], q_ref[:, at], halo_r[g, :, inner]], axis=0)
        return at, inner, query, ga[:, at], k_ref[:, at], v_ref[:, at]

    def first_pass(g, _):
        arrive(halo_copy, g)
        for part in range(GROUP):
            at, inner, query, grad, key, value = operands(g, part)
            scores = dot(key, query, 1, 1) * factor + bias[...]
            peak = jnp.max(scores, axis=0, keepdims=True)
            raised = jnp.exp(scores - peak)
            h = g * GROUP + part
            local[h, 0:1, :] = peak
            local[h, 1:2, :] = jnp.sum(raised, axis=0, keepdims=True)
            local[h, 2:3, :] = jnp.sum(raised * dot(value, grad, 1, 1), axis=0, keepdims=True)
        return 0

    def send_parts(b):
        for i in range(4):
            for j in range(3):
                row = local[b * 4 + i, j : j + 1, :]
                part_l[b, j * 4 + i : j * 4 + i + 1, :] = row[:, :low_end]
                part_r[b, j * 4 + i : j * 4 + i + 1, :] = row[:, high_end:]
        start(part_copy, b)

    def merge(b):
        arrive(part_copy, b)
        for i in range(4):
            def three(j, empty):
                pad = jnp.full((1, frames - WINDOW), empty, jnp.float32)
                at = slice(j * 4 + i, j * 4 + i + 1)
                return (
                    local[b * 4 + i, j : j + 1, low_end:high_end],
                    jnp.concatenate([got_l[b, at, :], pad], axis=1),
                    jnp.concatenate([pad, got_r[b, at, :]], axis=1),
                )

            peaks = three(0, NEG_FILL)
            peak = jnp.maximum(jnp.maximum(peaks[0], peaks[1]), peaks[2])
            scales = [jnp.exp(p - peak) for p in peaks]
            total = sum(a * c for a, c in zip(scales, three(1, 0.0)))
            drift = sum(a * c for a, c in zip(scales, three(2, 0.0))) / total
            level = peak + jnp.log(total)
            for j, row in ((0, level), (1, drift)):
                final[b * 4 + i, j : j + 1, low_end:high_end] = row
                done_l[b, j * 4 + i : j * 4 + i + 1, :] = row[:, :WINDOW]
                done_r[b, j * 4 + i : j * 4 + i + 1, :] = row[:, frames - WINDOW :]
        start(done_copy, b)

    def unpack(b):
        arrive(done_copy, b)
        for i in range(4):
            for j in range(2):
                at = slice(j * 4 + i, j * 4 + i + 1)
                final[b * 4 + i, j : j + 1, :low_end] = told_l[b, at, :]
                final[b * 4 + i, j : j + 1, high_end:] = told_r[b, at, :]

    def second_pass(g, _):
        for part in range(GROUP):
            at, inner, query, grad, key, value = operands(g, part)
            h = g * GROUP + part
            scores = dot(key, query, 1, 1) * factor + bias[...]
            probs = jnp.exp(scores - final[h, 0:1, :])
            low = probs.astype(jnp.bfloat16)
            dv_ref[:, at] = dot(low, grad, 1, 0).astype(jnp.bfloat16)
            att[:, at] = dot(low, value, 0, 0).astype(jnp.bfloat16)
            score_grad = (probs * (dot(value, grad, 1, 1) - final[h, 1:2, :])).astype(jnp.bfloat16)
            dk_ref[:, at] = (dot(score_grad, query, 1, 0) * factor).astype(jnp.bfloat16)
            total = dot(score_grad, key, 0, 0) * factor
            out_l[g, :, inner] = total[:low_end].astype(jnp.bfloat16)
            query_acc[:, at] = total[low_end:high_end]
            out_r[g, :, inner] = total[high_end:].astype(jnp.bfloat16)
        start(ret_copy, g)
        return 0

    lax.fori_loop(0, 2, first_pass, 0)
    send_parts(0)
    lax.fori_loop(2, 3, first_pass, 0)
    merge(0)
    lax.fori_loop(3, 4, first_pass, 0)
    send_parts(1)
    unpack(0)
    lax.fori_loop(0, 1, second_pass, 0)
    merge(1)
    lax.fori_loop(1, 2, second_pass, 0)
    unpack(1)
    lax.fori_loop(2, 4, second_pass, 0)

    if inside:
        wg, sums, send0, recv0, send1, recv1, send2, recv2, send3, recv3, send4, recv4, sc_send, sc_recv = scatter
        sends = (send0, send1, send2, send3, send4)
        recvs = (recv0, recv1, recv2, recv3, recv4)
    else:
        wg = wg_ref

    def weight(g, _):
        at = pl.ds(pl.multiple_of(g * cols, cols), cols)
        wg[:, at] = dot(gt[...], att[:, at], 1, 0)
        return 0

    lax.fori_loop(0, groups, weight, 0)

    if inside:
        block = wg_ref.shape[0]

        def exchange(step):
            return pltpu.make_async_remote_copy(
                src_ref=sends[step],
                dst_ref=recvs[step],
                send_sem=sc_send.at[step],
                recv_sem=sc_recv.at[step],
                device_id=partners[step],
                device_id_type=MESH,
            )

        def rows_of(s, c):
            return pl.ds(pl.multiple_of((s * 2 + c) * block, block), block)

        def pack0(s, _):
            send0[s] = wg[rows_of(s, 1 - core), :].astype(jnp.bfloat16)
            return 0

        lax.fori_loop(0, n, pack0, 0)
        exchange(0).start()
        exchange(0).wait_recv()

        def add0(s, _):
            sums[s] = wg[rows_of(s, core), :] + recv0[s].astype(jnp.float32)
            return 0

        lax.fori_loop(0, n, add0, 0)

        spots = (
            (8, lambda i, b: (i // 2) * 4 + b * 2 + lax.rem(i, 2), y),
            (4, lambda i, b: (i // 2) * 8 + b * 4 + y * 2 + lax.rem(i, 2), z0),
            (2, lambda i, b: b * 8 + z0 * 4 + y * 2 + i, z1),
            (1, lambda i, b: z1 * 8 + z0 * 4 + y * 2 + b + i * 0, x),
        )
        for t, (count, spot, bit) in enumerate(spots, 1):
            def pack(i, _):
                sends[t][i] = sums[spot(i, 1 - bit)].astype(jnp.bfloat16)
                return 0

            lax.fori_loop(0, count, pack, 0)
            exchange(t).start()
            exchange(t).wait_recv()

            def add(i, _):
                at = spot(i, bit)
                sums[at] = sums[at] + recvs[t][i].astype(jnp.float32)
                return 0

            lax.fori_loop(0, count, add, 0)
        wg_ref[...] = sums[me]
        for t in range(len(partners)):
            exchange(t).wait_send()

    def finish(g, _):
        arrive(ret_copy, g)
        sent(ret_copy, g)
        sent(halo_copy, g)
        at = pl.ds(pl.multiple_of(g * cols, cols), cols)
        pad = jnp.zeros((frames - WINDOW, cols), jnp.float32)
        total = query_acc[:, at]
        total = total + jnp.concatenate([ret_l[g].astype(jnp.float32), pad], axis=0)
        total = total + jnp.concatenate([pad, ret_r[g].astype(jnp.float32)], axis=0)
        dq_ref[:, at] = total.astype(jnp.bfloat16)
        return 0

    lax.fori_loop(0, groups, finish, 0)
    sent(grad_copy, 0)
    for b in range(2):
        sent(part_copy, b)
        sent(done_copy, b)


def body(n, dp, queries, keys, values, out_grad, proj_weight, lengths):
    frames, width = queries.shape[1:]
    head = width // HEADS
    cols = GROUP * head
    groups = HEADS // GROUP
    inside = n == 16 and dp == 2
    block = width // (n * dp)
    wide = frames + 2 * WINDOW
    bf16, f32 = jnp.bfloat16, jnp.float32
    edge = pltpu.VMEM((WINDOW, width), bf16)
    halo = pltpu.VMEM((groups, WINDOW, cols), bf16)
    stat = pltpu.VMEM((HEADS, 8, wide), f32)
    parts = pltpu.VMEM((2, 16, WINDOW), f32)
    done = pltpu.VMEM((2, 8, WINDOW), f32)
    one, some = pltpu.SemaphoreType.DMA((2,)), pltpu.SemaphoreType.DMA((2, groups))
    two = pltpu.SemaphoreType.DMA((2, 2))
    scratch = [
        pltpu.VMEM((frames, wide), f32),
        pltpu.VMEM((wide, width), bf16),
        pltpu.VMEM((width, wide), bf16),
        pltpu.VMEM((wide, width), bf16),
        pltpu.VMEM((frames, width), f32),
        edge, edge, halo, halo, halo, halo, halo, halo,
        stat, stat, parts, parts, parts, parts, done, done, done, done,
        one, one, some, some, some, some, two, two, two, two,
    ]
    if inside:
        scratch += [pltpu.VMEM((width, width), f32), pltpu.VMEM((n, block, width), f32)]
        for count in (16, 8, 4, 2, 1):
            scratch += [pltpu.VMEM((count, block, width), bf16)] * 2
        scratch += [pltpu.SemaphoreType.DMA((5,))] * 2
    wg_shape = (block, width) if inside else (width, width)
    vmem = pl.BlockSpec(memory_space=pltpu.VMEM)
    dq, dk, dv, wg = pl.pallas_call(
        functools.partial(kernel, n, inside),
        out_shape=[jax.ShapeDtypeStruct((frames, width), bf16)] * 3
        + [jax.ShapeDtypeStruct(wg_shape, f32)],
        in_specs=[vmem] * 6,
        out_specs=[vmem] * 4,
        scratch_shapes=scratch,
        compiler_params=pltpu.CompilerParams(
            collective_id=0, has_side_effects=True, vmem_limit_bytes=56 * 1024 * 1024
        ),
    )(queries[0], keys[0], values[0], out_grad[0], proj_weight, lengths)
    if not inside:
        wg = lax.psum_scatter(wg, ("seq", "dp"), scatter_dimension=0, tiled=True)
    return dq[None], dk[None], dv[None], wg


def solution(mesh):
    rows = P("dp", "seq", None)
    return jax.shard_map(
        functools.partial(body, mesh.shape["seq"], mesh.shape["dp"]),
        mesh=mesh,
        in_specs=(rows, rows, rows, rows, P(), P("dp", None)),
        out_specs=(rows, rows, rows, P(("seq", "dp"), None)),
        check_vma=False,
    )
```

```python
import functools

import jax
import jax.numpy as jnp
from jax import lax
from jax.experimental import pallas as pl
from jax.experimental.pallas import tpu as pltpu
from jax.sharding import PartitionSpec as P

HEADS = 8
WINDOW = 256
GROUP = 2
NEG_FILL = -1e30
MESH = pl.DeviceIdType.MESH


def dot(left, right, left_dim, right_dim):
    return lax.dot_general(
        left, right, (((left_dim,), (right_dim,)), ((), ())), preferred_element_type=jnp.float32
    )


def iota(shape, dim):
    return lax.broadcasted_iota(jnp.int32, shape, dim)


def fill_bias(bias, lengths_ref, me, frames):
    utts = lengths_ref.shape[1]
    lens = lengths_ref[...].astype(jnp.float32)
    upto = iota((utts, utts), 1) <= iota((utts, utts), 0)
    ends_col = jnp.sum(jnp.where(upto, lens, 0.0), axis=1, keepdims=True)
    same = iota((utts, utts), 1) == iota((utts, utts), 0)
    ends_row = jnp.sum(jnp.where(same, ends_col, 0.0), axis=0, keepdims=True)
    wide = bias.shape[1]
    last = ends_row[:, utts - 1 :]
    first = me * frames
    query_spots = first + iota((frames, 1), 0)
    key_spots = first - WINDOW + iota((1, wide), 1)
    query_at = query_spots.astype(jnp.float32)
    key_at = key_spots.astype(jnp.float32)
    query_seg = jnp.sum(jnp.where(ends_row <= query_at, 1.0, 0.0), axis=1, keepdims=True)
    key_seg = jnp.sum(jnp.where(ends_col <= key_at, 1.0, 0.0), axis=0, keepdims=True)
    key_seg = jnp.where((key_at >= 0.0) & (key_at < last), key_seg, -1.0)
    step = 128
    for r in range(0, frames, step):
        near = jnp.abs(query_at[r : r + step] - key_at) <= float(WINDOW)
        seen = near & (query_seg[r : r + step] == key_seg)
        bias[r : r + step, :] = jnp.where(seen, 0.0, NEG_FILL)


def kernel(
    n, inside,
    q_ref, k_ref, v_ref, g_ref, w_ref, lengths_ref,
    dq_ref, dk_ref, dv_ref, wg_ref,
    bias, ga, gt, att, query_acc,
    grad_l, grad_r, halo_l, halo_r, out_l, out_r, ret_l, ret_r,
    local, final, part_l, part_r, got_l, got_r, done_l, done_r, told_l, told_r,
    grad_send, grad_recv, halo_send, halo_recv, ret_send, ret_recv,
    part_send, part_recv, done_send, done_recv,
    *scatter,
):
    me = lax.axis_index("seq")
    core = lax.axis_index("dp")
    frames, width = q_ref.shape
    head = width // HEADS
    cols = GROUP * head
    groups = HEADS // GROUP
    factor = head ** (-0.5)
    has_l = me > 0
    has_r = me < n - 1
    left = jnp.maximum(me - 1, 0)
    right = jnp.minimum(me + 1, n - 1)
    low_end, high_end = WINDOW, WINDOW + frames
    if inside:
        x, y = lax.rem(me, 2), lax.rem(me // 2, 2)
        z0, z1 = lax.rem(me // 4, 2), me // 8
        partners = (
            (me, 1 - core),
            (me + 2 - 4 * y, core),
            (me + 4 - 8 * z0, core),
            (me + 8 - 16 * z1, core),
            (me + 1 - 2 * x, core),
        )
    else:
        partners = ()

    barrier = pltpu.get_barrier_semaphore()

    @pl.when(has_l)
    def _():
        pl.semaphore_signal(barrier, inc=1, device_id=(left, core), device_id_type=MESH)

    @pl.when(has_r)
    def _():
        pl.semaphore_signal(barrier, inc=1, device_id=(right, core), device_id_type=MESH)

    for partner in partners:
        pl.semaphore_signal(barrier, inc=1, device_id=partner, device_id_type=MESH)
    greeted = jnp.where(has_l, 1, 0) + jnp.where(has_r, 1, 0) + len(partners)
    pl.semaphore_wait(barrier, greeted)

    edges = (pl.ds(0, WINDOW), pl.ds(frames - WINDOW, WINDOW))

    def copy(side, src, dst, send, recv):
        return pltpu.make_async_remote_copy(
            src_ref=src,
            dst_ref=dst,
            send_sem=send,
            recv_sem=recv,
            device_id=((left, right)[side], core),
            device_id_type=MESH,
        )

    def grad_copy(side, _):
        return copy(side, g_ref.at[edges[side], :], (grad_r, grad_l)[side],
                    grad_send.at[side], grad_recv.at[side])

    def halo_copy(side, g):
        at = pl.ds(pl.multiple_of(g * cols, cols), cols)
        return copy(side, q_ref.at[edges[side], at], (halo_r, halo_l)[side].at[g],
                    halo_send.at[side, g], halo_recv.at[side, g])

    def part_copy(side, b):
        return copy(side, (part_l, part_r)[side].at[b], (got_r, got_l)[side].at[b],
                    part_send.at[side, b], part_recv.at[side, b])

    def done_copy(side, b):
        return copy(side, (done_l, done_r)[side].at[b], (told_r, told_l)[side].at[b],
                    done_send.at[side, b], done_recv.at[side, b])

    def ret_copy(side, g):
        return copy(side, (out_l, out_r)[side].at[g], (ret_r, ret_l)[side].at[g],
                    ret_send.at[side, g], ret_recv.at[side, g])

    def start(make, i):
        @pl.when(has_l)
        def _():
            make(0, i).start()

        @pl.when(has_r)
        def _():
            make(1, i).start()

    def arrive(make, i):
        @pl.when(has_l)
        def _():
            make(1, i).wait_recv()

        @pl.when(has_r)
        def _():
            make(0, i).wait_recv()

    def sent(make, i):
        @pl.when(has_l)
        def _():
            make(0, i).wait_send()

        @pl.when(has_r)
        def _():
            make(1, i).wait_send()

    start(grad_copy, 0)

    def start_halos(g, _):
        start(halo_copy, g)
        return 0

    lax.fori_loop(0, groups, start_halos, 0)

    blank = jnp.where(iota((2, 16, WINDOW), 1) < 4, NEG_FILL, 0.0)

    @pl.when(jnp.logical_not(has_l))
    def _():
        for ref in (grad_l, halo_l, ret_l, told_l):
            ref[...] = jnp.zeros_like(ref)
        got_l[...] = blank

    @pl.when(jnp.logical_not(has_r))
    def _():
        for ref in (grad_r, halo_r, ret_r, told_r):
            ref[...] = jnp.zeros_like(ref)
        got_r[...] = blank

    fill_bias(bias, lengths_ref, me, frames)
    part_l[...] = jnp.zeros_like(part_l)
    part_r[...] = jnp.zeros_like(part_r)

    def project(ref, first, rows):
        gt[:, first : first + rows] = ref[...].T

        def some(g, _):
            at = pl.ds(pl.multiple_of(g * cols, cols), cols)
            ga[first : first + rows, at] = dot(ref[...], w_ref[:, at], 1, 0).astype(jnp.bfloat16)
            return 0

        lax.fori_loop(0, groups, some, 0)

    project(g_ref, low_end, frames)
    arrive(grad_copy, 0)
    project(grad_l, 0, WINDOW)
    project(grad_r, high_end, WINDOW)

    def operands(g, part):
        at = pl.ds(pl.multiple_of(g * cols + part * head, head), head)
        inner = slice(part * head, (part + 1) * head)
        query = jnp.concatenate([halo_l[g, :, inner], q_ref[:, at], halo_r[g, :, inner]], axis=0)
        return at, inner, query, ga[:, at], k_ref[:, at], v_ref[:, at]

    def first_pass(g, _):
        arrive(halo_copy, g)
        for part in range(GROUP):
            at, inner, query, grad, key, value = operands(g, part)
            scores = dot(key, query, 1, 1) * factor + bias[...]
            peak = jnp.max(scores, axis=0, keepdims=True)
            raised = jnp.exp(scores - peak)
            h = g * GROUP + part
            local[h, 0:1, :] = peak
            local[h, 1:2, :] = jnp.sum(raised, axis=0, keepdims=True)
            local[h, 2:3, :] = jnp.sum(raised * dot(value, grad, 1, 1), axis=0, keepdims=True)
        return 0

    def send_parts(b):
        for i in range(4):
            for j in range(3):
                row = local[b * 4 + i, j : j + 1, :]
                part_l[b, j * 4 + i : j * 4 + i + 1, :] = row[:, :low_end]
                part_r[b, j * 4 + i : j * 4 + i + 1, :] = row[:, high_end:]
        start(part_copy, b)

    def merge(b):
        arrive(part_copy, b)
        for i in range(4):
            def three(j, empty):
                pad = jnp.full((1, frames - WINDOW), empty, jnp.float32)
                at = slice(j * 4 + i, j * 4 + i + 1)
                return (
                    local[b * 4 + i, j : j + 1, low_end:high_end],
                    jnp.concatenate([got_l[b, at, :], pad], axis=1),
                    jnp.concatenate([pad, got_r[b, at, :]], axis=1),
                )

            peaks = three(0, NEG_FILL)
            peak = jnp.maximum(jnp.maximum(peaks[0], peaks[1]), peaks[2])
            scales = [jnp.exp(p - peak) for p in peaks]
            total = sum(a * c for a, c in zip(scales, three(1, 0.0)))
            drift = sum(a * c for a, c in zip(scales, three(2, 0.0))) / total
            level = peak + jnp.log(total)
            for j, row in ((0, level), (1, drift)):
                final[b * 4 + i, j : j + 1, low_end:high_end] = row
                done_l[b, j * 4 + i : j * 4 + i + 1, :] = row[:, :WINDOW]
                done_r[b, j * 4 + i : j * 4 + i + 1, :] = row[:, frames - WINDOW :]
        start(done_copy, b)

    def unpack(b):
        arrive(done_copy, b)
        for i in range(4):
            for j in range(2):
                at = slice(j * 4 + i, j * 4 + i + 1)
                final[b * 4 + i, j : j + 1, :low_end] = told_l[b, at, :]
                final[b * 4 + i, j : j + 1, high_end:] = told_r[b, at, :]

    def second_pass(g, _):
        for part in range(GROUP):
            at, inner, query, grad, key, value = operands(g, part)
            h = g * GROUP + part
            scores = dot(key, query, 1, 1) * factor + bias[...]
            probs = jnp.exp(scores - final[h, 0:1, :])
            low = probs.astype(jnp.bfloat16)
            dv_ref[:, at] = dot(low, grad, 1, 0).astype(jnp.bfloat16)
            att[:, at] = dot(low, value, 0, 0).astype(jnp.bfloat16)
            score_grad = (probs * (dot(value, grad, 1, 1) - final[h, 1:2, :])).astype(jnp.bfloat16)
            dk_ref[:, at] = (dot(score_grad, query, 1, 0) * factor).astype(jnp.bfloat16)
            total = dot(score_grad, key, 0, 0) * factor
            out_l[g, :, inner] = total[:low_end].astype(jnp.bfloat16)
            query_acc[:, at] = total[low_end:high_end]
            out_r[g, :, inner] = total[high_end:].astype(jnp.bfloat16)
        start(ret_copy, g)
        return 0

    if inside:
        wg, sums, send0, recv0, send1, recv1, send2, recv2, send3, recv3, send4, recv4, sc_send, sc_recv = scatter
        sends = (send0, send1, send2, send3, send4)
        recvs = (recv0, recv1, recv2, recv3, recv4)
    else:
        wg = wg_ref
    block = wg_ref.shape[0]
    half = width // 2

    def weight(b):
        def some(g, _):
            at = pl.ds(pl.multiple_of(g * cols, cols), cols)
            wg[:, at] = dot(gt[...], att[:, at], 1, 0)
            return 0

        lax.fori_loop(b * 2, b * 2 + 2, some, 0)

    def exchange(t, b):
        return pltpu.make_async_remote_copy(
            src_ref=sends[t].at[b],
            dst_ref=recvs[t].at[b],
            send_sem=sc_send.at[t, b],
            recv_sem=sc_recv.at[t, b],
            device_id=partners[t],
            device_id_type=MESH,
        )

    def rows_of(s, c):
        return pl.ds(pl.multiple_of((s * 2 + c) * block, block), block)

    if inside:
        spots = (
            (n, None, None),
            (8, lambda i, b: (i // 2) * 4 + b * 2 + lax.rem(i, 2), y),
            (4, lambda i, b: (i // 2) * 8 + b * 4 + y * 2 + lax.rem(i, 2), z0),
            (2, lambda i, b: b * 8 + z0 * 4 + y * 2 + i, z1),
            (1, lambda i, b: z1 * 8 + z0 * 4 + y * 2 + b + i * 0, x),
        )

    def begin(t, b):
        if not inside:
            return
        count, spot, bit = spots[t]
        at = slice(b * half, (b + 1) * half)

        def pack(i, _):
            if t == 0:
                sends[0][b, i] = wg[rows_of(i, 1 - core), at].astype(jnp.bfloat16)
            else:
                sends[t][b, i] = sums[spot(i, 1 - bit), :, at].astype(jnp.bfloat16)
            return 0

        lax.fori_loop(0, count, pack, 0)
        exchange(t, b).start()

    def end(t, b):
        if not inside:
            return
        count, spot, bit = spots[t]
        at = slice(b * half, (b + 1) * half)
        exchange(t, b).wait_recv()

        def add(i, _):
            if t == 0:
                sums[i, :, at] = wg[rows_of(i, core), at] + recvs[0][b, i].astype(jnp.float32)
            else:
                to = spot(i, bit)
                sums[to, :, at] = sums[to, :, at] + recvs[t][b, i].astype(jnp.float32)
            return 0

        lax.fori_loop(0, count, add, 0)

    lax.fori_loop(0, 2, first_pass, 0)
    send_parts(0)
    lax.fori_loop(2, 3, first_pass, 0)
    merge(0)
    lax.fori_loop(3, 4, first_pass, 0)
    send_parts(1)
    unpack(0)
    lax.fori_loop(0, 1, second_pass, 0)
    merge(1)
    lax.fori_loop(1, 2, second_pass, 0)
    weight(0)
    begin(0, 0)
    unpack(1)
    lax.fori_loop(2, 3, second_pass, 0)
    end(0, 0)
    begin(1, 0)
    lax.fori_loop(3, 4, second_pass, 0)
    weight(1)
    begin(0, 1)
    end(1, 0)
    begin(2, 0)
    end(0, 1)
    begin(1, 1)
    end(2, 0)
    begin(3, 0)
    end(3, 0)
    begin(4, 0)
    end(1, 1)
    begin(2, 1)
    end(4, 0)
    end(2, 1)
    begin(3, 1)
    end(3, 1)
    begin(4, 1)
    end(4, 1)
    if inside:
        wg_ref[...] = sums[me]
        for t in range(len(partners)):
            exchange(t, 0).wait_send()
            exchange(t, 1).wait_send()

    def finish(g, _):
        arrive(ret_copy, g)
        sent(ret_copy, g)
        sent(halo_copy, g)
        at = pl.ds(pl.multiple_of(g * cols, cols), cols)
        pad = jnp.zeros((frames - WINDOW, cols), jnp.float32)
        total = query_acc[:, at]
        total = total + jnp.concatenate([ret_l[g].astype(jnp.float32), pad], axis=0)
        total = total + jnp.concatenate([pad, ret_r[g].astype(jnp.float32)], axis=0)
        dq_ref[:, at] = total.astype(jnp.bfloat16)
        return 0

    lax.fori_loop(0, groups, finish, 0)
    sent(grad_copy, 0)
    for b in range(2):
        sent(part_copy, b)
        sent(done_copy, b)


def body(n, dp, queries, keys, values, out_grad, proj_weight, lengths):
    frames, width = queries.shape[1:]
    head = width // HEADS
    cols = GROUP * head
    groups = HEADS // GROUP
    inside = n == 16 and dp == 2
    block = width // (n * dp)
    wide = frames + 2 * WINDOW
    bf16, f32 = jnp.bfloat16, jnp.float32
    edge = pltpu.VMEM((WINDOW, width), bf16)
    halo = pltpu.VMEM((groups, WINDOW, cols), bf16)
    stat = pltpu.VMEM((HEADS, 8, wide), f32)
    parts = pltpu.VMEM((2, 16, WINDOW), f32)
    done = pltpu.VMEM((2, 8, WINDOW), f32)
    one, some = pltpu.SemaphoreType.DMA((2,)), pltpu.SemaphoreType.DMA((2, groups))
    two = pltpu.SemaphoreType.DMA((2, 2))
    scratch = [
        pltpu.VMEM((frames, wide), f32),
        pltpu.VMEM((wide, width), bf16),
        pltpu.VMEM((width, wide), bf16),
        pltpu.VMEM((wide, width), bf16),
        pltpu.VMEM((frames, width), f32),
        edge, edge, halo, halo, halo, halo, halo, halo,
        stat, stat, parts, parts, parts, parts, done, done, done, done,
        one, one, some, some, some, some, two, two, two, two,
    ]
    if inside:
        scratch += [pltpu.VMEM((width, width), f32), pltpu.VMEM((n, block, width), f32)]
        for count in (16, 8, 4, 2, 1):
            scratch += [pltpu.VMEM((2, count, block, width // 2), bf16)] * 2
        scratch += [pltpu.SemaphoreType.DMA((5, 2))] * 2
    wg_shape = (block, width) if inside else (width, width)
    vmem = pl.BlockSpec(memory_space=pltpu.VMEM)
    dq, dk, dv, wg = pl.pallas_call(
        functools.partial(kernel, n, inside),
        out_shape=[jax.ShapeDtypeStruct((frames, width), bf16)] * 3
        + [jax.ShapeDtypeStruct(wg_shape, f32)],
        in_specs=[vmem] * 6,
        out_specs=[vmem] * 4,
        scratch_shapes=scratch,
        compiler_params=pltpu.CompilerParams(
            collective_id=0, has_side_effects=True, vmem_limit_bytes=56 * 1024 * 1024
        ),
    )(queries[0], keys[0], values[0], out_grad[0], proj_weight, lengths)
    if not inside:
        wg = lax.psum_scatter(wg, ("seq", "dp"), scatter_dimension=0, tiled=True)
    return dq[None], dk[None], dv[None], wg


def solution(mesh):
    rows = P("dp", "seq", None)
    return jax.shard_map(
        functools.partial(body, mesh.shape["seq"], mesh.shape["dp"]),
        mesh=mesh,
        in_specs=(rows, rows, rows, rows, P(), P("dp", None)),
        out_specs=(rows, rows, rows, P(("seq", "dp"), None)),
        check_vma=False,
    )
```
